256 devices in a mesh: row: 4 (over x_lo, core), col: 16 (over z, x_hi), layer: 4 (over y).
Axes of the slice: x: 4 (x_hi: 2, x_lo: 2; x = x_hi * 2 + x_lo), y: 4, z: 8, core: 2. Of those that a mesh axis runs over, the one named last changes fastest.
Arguments:
- left_values: float32 [4, 8192, 4096], P('layer', 'row', 'col'), may hold values from -6 to 6
- left_pattern: int32 [4, 64, 32], P('layer', 'row', 'col'), may hold values from 0 to 1, as said below
- right_values: float32 [4, 4096, 4096], P('layer', 'row', 'col'), may hold values from -0.046875 to 0.046875
- right_pattern: int32 [4, 32, 32], P('layer', 'row', 'col'), may hold values from 0 to 1, as said below
Outputs:
- product: float32 [8192, 4096], P(('row', 'layer'), 'col')
The draws below stay inside these ranges and needn't reach their ends.
Inputs may be any that keep to these rules, and one draw needn't show every extreme that they name: `left_pattern`: 1 marks an occupied block, 0 an empty one. `right_pattern`: 1 marks an occupied block, 0 an empty one.
All inputs are finite; a program needn't handle non-finite values.
Results may differ from the reference program's by a relative error of at most 0.0001.
Values sent between devices are 32-bit elements; how exact they have to be, the bound alone decides.
No kernel may reach another device: no remote copies, remote signals or barrier semaphores. Data moves between devices by JAX's collectives and lax.ppermute only.
A program may use at most 128 MiB of HBM per device.

```python
import jax
import jax.numpy as jnp
from jax import lax

BS = 128
LAYERS = 4
M = 8192
KL = 4096
K = 16384
N = 4096


def band_pattern(key, lead_count, lead_total, trail_count, lead_inner):
    first = jnp.arange(lead_count, dtype=jnp.int32)
    second = jnp.arange(trail_count, dtype=jnp.int32)
    slabs = jnp.arange(LAYERS, dtype=jnp.int32)
    if lead_inner:
        inner = slabs[:, None, None] * lead_count + first[None, :, None]
        other = second[None, None, :]
        center = other * (LAYERS * lead_count) // trail_count
        shape = (LAYERS, lead_count, trail_count)
    else:
        inner = slabs[:, None, None] * trail_count + second[None, None, :]
        other = first[None, :, None]
        center = other * (LAYERS * trail_count) // lead_count
        shape = (LAYERS, lead_count, trail_count)
    reach = max(lead_total // 4, 1)
    inside = jnp.abs(inner - center) <= reach
    extra = jax.random.randint(key, shape, 0, 8) == 0
    return jnp.logical_or(inside, extra).astype(jnp.int32)


def draw_left_pattern(key, part):
    key = jax.random.fold_in(key, 11)
    rows = M // BS
    inner = KL // BS
    return band_pattern(key, rows, LAYERS * inner, inner, False)


def draw_right_pattern(key, part):
    key = jax.random.fold_in(key, 23)
    inner = KL // BS
    columns = N // BS
    return band_pattern(key, inner, LAYERS * inner, columns, True)


def shard_levels(stream_key, extent, shards, smallest, top_value):
    loudness, own = 1.0, jax.random.fold_in(stream_key, 6)
    for axis_at, blocks in shards:
        heights = jnp.exp(jax.random.uniform(jax.random.fold_in(own, axis_at), (blocks,), jnp.float32, smallest / len(shards), top_value / len(shards)))
        loudness = loudness * jnp.repeat(heights, extent[axis_at] // blocks).reshape([-1 if axis == axis_at else 1 for axis in range(len(extent))])
    return loudness


def gaussian(stream_key, shape, scale, most, shards=(), held_as=jnp.bfloat16):
    values = jax.random.normal(stream_key, shape, jnp.float32) * scale
    if len(shards) > 0:
        values = shard_levels(stream_key, shape, shards, -0.22, 0.18) * values
    return jnp.clip(values, min=-most, max=most).astype(held_as)


def setup_inputs(seed: int = 0) -> dict:
    key_list = jax.random.split(jax.random.key(seed), 5)
    return {
        "left_values": gaussian(key_list[0], (LAYERS, M, KL), 1.0, 6.0, ((0, 4), (1, 4), (2, 16)), jnp.float32),
        "left_pattern": draw_left_pattern(jax.random.fold_in(key_list[4], 71), 0),
        "right_values": gaussian(key_list[2], (LAYERS, KL, N), K ** -0.5, 0.046875, ((0, 4), (1, 4), (2, 16)), jnp.float32),
        "right_pattern": draw_right_pattern(jax.random.fold_in(key_list[4], 71), 0),
    }


def spread(pattern, size):
    return jnp.repeat(jnp.repeat(pattern, size, axis=0), size, axis=1).astype(jnp.float32)


def reference(left_values, left_pattern, right_values, right_pattern):
    total = jnp.zeros((M, N), jnp.float32)
    for slab in range(LAYERS):
        left = left_values[slab] * spread(left_pattern[slab], BS)
        right = right_values[slab] * spread(right_pattern[slab], BS)
        total = total + jnp.dot(left, right, preferred_element_type=jnp.float32, precision=lax.Precision.HIGHEST)
    return total
```

```python
import jax
import jax.numpy as jnp
from jax import lax
from jax.experimental import pallas as pl
from jax.experimental.pallas import tpu as pltpu
from jax.sharding import Mesh, PartitionSpec as P

BS = 128
F32 = jnp.float32
BF16 = jnp.bfloat16
VMEM_BYTES = 48 * 1024 * 1024


def mask_left_kernel(pattern_ref, values_ref, out_ref):
    at = pl.program_id(0)
    for i in range(2):
        for j in range(2):
            rows, columns = slice(i * BS, (i + 1) * BS), slice(j * BS, (j + 1) * BS)
            keep = pattern_ref[2 * at + i, j].astype(F32)
            out_ref[rows, columns] = values_ref[rows, columns] * keep


def mask_left(values, pattern):
    rows = values.shape[0]
    return pl.pallas_call(
        mask_left_kernel,
        grid=(rows // 256,),
        in_specs=[
            pl.BlockSpec(memory_space=pltpu.SMEM),
            pl.BlockSpec((256, 256), lambda i: (i, 0)),
        ],
        out_specs=pl.BlockSpec((256, 256), lambda i: (i, 0)),
        out_shape=jax.ShapeDtypeStruct(values.shape, F32),
        cost_estimate=pl.CostEstimate(flops=values.size, bytes_accessed=8 * values.size, transcendentals=0),
    )(pattern, values)


def mask_right_kernel(pattern_ref, values_ref, out_ref):
    at = pl.program_id(0)
    for h in range(4):
        for j in range(2):
            columns = slice(j * BS, (j + 1) * BS)
            keep = pattern_ref[2 * at + h // 2, j].astype(F32)
            out_ref[h, 0, :, columns] = values_ref[h * 64 : (h + 1) * 64, columns] * keep


def mask_right(values, pattern):
    return pl.pallas_call(
        mask_right_kernel,
        grid=(4,),
        in_specs=[
            pl.BlockSpec(memory_space=pltpu.SMEM),
            pl.BlockSpec((256, 256), lambda i: (i, 0)),
        ],
        out_specs=pl.BlockSpec((4, 1, 64, 256), lambda i: (0, i, 0, 0)),
        out_shape=jax.ShapeDtypeStruct((4, 4, 64, 256), F32),
        cost_estimate=pl.CostEstimate(flops=values.size, bytes_accessed=8 * values.size, transcendentals=0),
    )(pattern, values)


def prepare_kernel(where_ref, b0_ref, b1_ref, b2_ref, b3_ref, high_ref, low_ref):
    xh = where_ref[8]
    for i, ref in enumerate((b0_ref, b1_ref, b2_ref, b3_ref)):
        rows = pl.ds(pl.multiple_of(where_ref[4 + i] * 64, 64), 64)
        for z0 in range(2):
            for near in range(2):
                block = ref[2 * z0 + lax.bitwise_xor(xh, jnp.int32(near))]
                high = block.astype(BF16)
                low = (block - high.astype(F32)).astype(BF16)
                columns = slice(z0 * 512 + near * 256, z0 * 512 + near * 256 + 256)
                high_ref[rows, columns] = high
                low_ref[rows, columns] = low


def prepare(where, parts):
    spec = pl.BlockSpec((4, 64, 256), lambda t, s: (s[t], 0, 0))
    out = pl.BlockSpec((256, 1024), lambda t, s: (t, 0))
    return pl.pallas_call(
        prepare_kernel,
        grid_spec=pltpu.PrefetchScalarGridSpec(
            num_scalar_prefetch=1, grid=(4,), in_specs=[spec] * 4, out_specs=[out] * 2
        ),
        out_shape=[jax.ShapeDtypeStruct((1024, 1024), BF16)] * 2,
        cost_estimate=pl.CostEstimate(flops=3 << 20, bytes_accessed=8 << 20, transcendentals=0),
    )(where, *parts)


def split(block):
    high = block.astype(BF16)
    return high, (block - high.astype(F32)).astype(BF16)


def product_kernel(a0_ref, a1_ref, a2_ref, a3_ref, high_ref, low_ref, *out_refs):
    pieces = [split(ref[...]) for ref in (a0_ref, a1_ref, a2_ref, a3_ref)]
    high = jnp.concatenate([p[0] for p in pieces], axis=1)
    low = jnp.concatenate([p[1] for p in pieces], axis=1)
    for z0 in range(2):
        columns = slice(z0 * 512, (z0 + 1) * 512)
        terms = jnp.dot(low, high_ref[:, columns], preferred_element_type=F32)
        terms += jnp.dot(high, low_ref[:, columns], preferred_element_type=F32)
        terms += jnp.dot(high, high_ref[:, columns], preferred_element_type=F32)
        if len(out_refs) == 1:
            out_refs[0][z0] = terms
        else:
            out_refs[0][z0] = terms[:, :256]
            out_refs[1][z0] = terms[:, 256:]


def partial_product(blocks, high, low, half, n_out):
    width = 512 // n_out
    return pl.pallas_call(
        product_kernel,
        grid=(4,),
        in_specs=[pl.BlockSpec((256, 256), lambda i: (2 * i + half, 0))] * 4
        + [pl.BlockSpec((1024, 1024), lambda i: (0, 0))] * 2,
        out_specs=[pl.BlockSpec((2, 256, width), lambda i: (i, 0, 0))] * n_out,
        out_shape=[jax.ShapeDtypeStruct((8, 256, width), F32)] * n_out,
        compiler_params=pltpu.CompilerParams(vmem_limit_bytes=VMEM_BYTES),
        cost_estimate=pl.CostEstimate(flops=6 << 30, bytes_accessed=12 << 20, transcendentals=0),
    )(*blocks, high, low)


def swap(value, axis):
    return lax.ppermute(value, axis, [(0, 1), (1, 0)])


def body(left_values, left_pattern, right_values, right_pattern):
    xl, core, xh, y = (lax.axis_index(n) for n in ("xl", "core", "xh", "y"))
    turn = 1 - 2 * core
    where = jnp.stack(
        [(y - turn * t + 4) % 4 for t in range(4)]
        + [2 * xl + core, 2 * (1 - xl) + core, 2 * xl + 1 - core, 2 * (1 - xl) + 1 - core, xh]
    ).astype(jnp.int32)

    left = mask_left(left_values[0], left_pattern[0])
    right = mask_right(right_values[0], right_pattern[0])

    ring = [(c * 4 + i, c * 4 + (i + 1 - 2 * c) % 4) for c in range(2) for i in range(4)]
    blocks = [left]
    for _ in range(3):
        blocks.append(lax.ppermute(blocks[-1], ("core", "y"), ring))

    right = right.reshape(16, 64, 256)
    right = lax.all_to_all(right, ("xl", "core"), split_axis=0, concat_axis=0, tiled=True)
    right = lax.all_to_all(right, ("z", "xh"), split_axis=0, concat_axis=0, tiled=True)
    right = lax.all_to_all(right, "y", split_axis=0, concat_axis=0, tiled=True)
    right_far = swap(right, "xl")
    parts = (right, right_far, swap(right, "core"), swap(right_far, "core"))
    high, low = prepare(where, parts)

    keep, send = partial_product(blocks, high, low, 1, 2)
    (both,) = partial_product(blocks, high, low, 0, 1)
    got = swap(send, "xh")
    second = lax.psum_scatter(keep + got, "z", scatter_dimension=0, tiled=True)[0]
    first = lax.psum_scatter(both, "z", scatter_dimension=0, tiled=True)[0]
    first = first[:, :256] + swap(first[:, 256:], "xh")

    turned = [
        ((2 * b + z0) * 4 + a, (2 * a + z0) * 4 + b) for a in range(4) for b in range(4) for z0 in range(2)
    ]
    mine = jnp.concatenate([first, second], axis=0)
    return lax.ppermute(mine, ("z", "y"), turned)


def solution(mesh):
    fine = Mesh(mesh.devices.reshape(2, 2, 8, 2, 4), ("xl", "core", "z", "xh", "y"))
    spec = P("y", ("xl", "core"), ("z", "xh"))
    return jax.shard_map(
        body,
        mesh=fine,
        in_specs=(spec,) * 4,
        out_specs=P(("xl", "core", "y"), ("z", "xh")),
        check_vma=False,
    )
```

```python
import jax
import jax.numpy as jnp
from jax import lax
from jax.experimental import pallas as pl
from jax.experimental.pallas import tpu as pltpu
from jax.sharding import Mesh, PartitionSpec as P

BS = 128
F32 = jnp.float32
BF16 = jnp.bfloat16
VMEM_BYTES = 48 * 1024 * 1024


def cost(flops, bytes_accessed):
    return pl.CostEstimate(flops=flops, bytes_accessed=bytes_accessed, transcendentals=0)


def mask_right_kernel(pattern_ref, values_ref, out_ref):
    at = pl.program_id(0)
    for h in range(4):
        for j in range(2):
            keep = pattern_ref[(2 * at + h // 2) * 2 + j].astype(F32)
            for i in range(2):
                columns = slice(j * BS + i * 64, j * BS + i * 64 + 64)
                top = values_ref[h * 64 : h * 64 + 32, columns]
                bottom = values_ref[h * 64 + 32 : h * 64 + 64, columns]
                out_ref[h, 0, 2 * j + i] = jnp.concatenate([top, bottom], axis=1) * keep


def mask_right(values, pattern):
    return pl.pallas_call(
        mask_right_kernel,
        grid=(4,),
        in_specs=[
            pl.BlockSpec(memory_space=pltpu.SMEM),
            pl.BlockSpec((256, 256), lambda i: (i, 0)),
        ],
        out_specs=pl.BlockSpec((4, 1, 4, 32, 128), lambda i: (0, i, 0, 0, 0)),
        out_shape=jax.ShapeDtypeStruct((4, 4, 4, 32, 128), F32),
        cost_estimate=cost(values.size, 8 * values.size),
    )(pattern.reshape(16), values)


def prepare_kernel(where_ref, b0_ref, b1_ref, b2_ref, b3_ref, high_ref, low_ref):
    xh = where_ref[8]
    for i, ref in enumerate((b0_ref, b1_ref, b2_ref, b3_ref)):
        base = where_ref[4 + i] * 64
        for near in range(2):
            nx = lax.bitwise_xor(xh, jnp.int32(near))
            for pair in range(4):
                even, odd = ref[2 * pair, nx, 0], ref[2 * pair + 1, nx, 0]
                columns = slice(near * 512 + pair * 128, near * 512 + pair * 128 + 128)
                for half in range(2):
                    lanes = slice(half * 64, half * 64 + 64)
                    block = jnp.concatenate([even[:, lanes], odd[:, lanes]], axis=1)
                    high = block.astype(BF16)
                    rows = pl.ds(pl.multiple_of(base + half * 32, 32), 32)
                    high_ref[rows, columns] = high
                    low_ref[rows, columns] = (block - high.astype(F32)).astype(BF16)


def prepare(where, parts):
    spec = pl.BlockSpec((8, 2, 1, 32, 128), lambda t, s: (0, 0, s[t], 0, 0))
    out = pl.BlockSpec((256, 1024), lambda t, s: (t, 0))
    return pl.pallas_call(
        prepare_kernel,
        grid_spec=pltpu.PrefetchScalarGridSpec(
            num_scalar_prefetch=1, grid=(4,), in_specs=[spec] * 4, out_specs=[out] * 2
        ),
        out_shape=[jax.ShapeDtypeStruct((1024, 1024), BF16)] * 2,
        cost_estimate=cost(3 << 20, 8 << 20),
    )(where, *[p.reshape(8, 2, 4, 32, 128) for p in parts])


def product_kernel(half, where_ref, pattern_ref, a0_ref, a1_ref, a2_ref, a3_ref, high_ref, low_ref, out_ref):
    my = pl.program_id(0)
    highs, lows = [], []
    for t, ref in enumerate((a0_ref, a1_ref, a2_ref, a3_ref)):
        rows = []
        for i in range(2):
            row = []
            for j in range(2):
                at = where_ref[t] * 32 + (my * 4 + half * 2 + i) * 2 + j
                row.append(ref[i * BS : (i + 1) * BS, j * BS : (j + 1) * BS] * pattern_ref[at].astype(F32))
            rows.append(jnp.concatenate(row, axis=1))
        block = jnp.concatenate(rows, axis=0)
        high = block.astype(BF16)
        highs.append(high)
        lows.append((block - high.astype(F32)).astype(BF16))
    high = jnp.concatenate(highs, axis=1)
    low = jnp.concatenate(lows, axis=1)
    for near in range(out_ref.shape[1]):
        columns = slice(near * 512, near * 512 + 512)
        terms = jnp.dot(low, high_ref[:, columns], preferred_element_type=F32)
        terms += jnp.dot(high, low_ref[:, columns], preferred_element_type=F32)
        terms += jnp.dot(high, high_ref[:, columns], preferred_element_type=F32)
        for nz in range(8):
            lanes = slice(nz * 64, nz * 64 + 64)
            out_ref[nz, near] = jnp.concatenate([terms[:128, lanes], terms[128:, lanes]], axis=1)


def partial_product(where, pattern, blocks, high, low, half, nears):
    first, count = nears[0], len(nears)
    smem = pl.BlockSpec(memory_space=pltpu.SMEM)
    return pl.pallas_call(
        lambda *refs: product_kernel(half, *refs),
        grid=(4,),
        in_specs=[smem, smem]
        + [pl.BlockSpec((256, 256), lambda i: (2 * i + half, 0))] * 4
        + [pl.BlockSpec((1024, 512 * count), lambda i: (0, first))] * 2,
        out_specs=pl.BlockSpec((8, count, 128, 128), lambda i: (0, 0, i, 0)),
        out_shape=jax.ShapeDtypeStruct((8, count, 512, 128), F32),
        compiler_params=pltpu.CompilerParams(vmem_limit_bytes=VMEM_BYTES),
        cost_estimate=cost((3 << 30) * count, (6 << 20) + (4 << 20) * count),
    )(where, pattern, *blocks, high, low)


def assemble_kernel(first_ref, second_ref, out_ref):
    for half, ref in enumerate((first_ref, second_ref)):
        for lane in range(2):
            rows = slice(half * 256 + lane * 128, half * 256 + lane * 128 + 128)
            lanes = slice(lane * 64, lane * 64 + 64)
            for pair in range(2):
                left, right = ref[2 * pair, :, lanes], ref[2 * pair + 1, :, lanes]
                out_ref[rows, pair * 128 : pair * 128 + 128] = jnp.concatenate([left, right], axis=1)


def assemble(first, second):
    return pl.pallas_call(
        assemble_kernel,
        out_shape=jax.ShapeDtypeStruct((512, 256), F32),
        cost_estimate=cost(0, 1 << 20),
    )(first.reshape(4, 128, 128), second.reshape(4, 128, 128))


def swap(value, axis):
    return lax.ppermute(value, axis, [(0, 1), (1, 0)])


def to_all(value, axis):
    return lax.all_to_all(value, axis, split_axis=0, concat_axis=0, tiled=True)


def body(left_values, left_pattern, right_values, right_pattern):
    xl, core, xh, y = (lax.axis_index(n) for n in ("xl", "core", "xh", "y"))
    turn = 1 - 2 * core
    where = jnp.stack(
        [(y - turn * t + 4) % 4 for t in range(4)]
        + [2 * xl + core, 2 * (1 - xl) + core, 2 * xl + 1 - core, 2 * (1 - xl) + 1 - core, xh]
    ).astype(jnp.int32)

    pattern = lax.all_gather(left_pattern.reshape(32), "y", axis=0, tiled=True)
    ring = [(c * 4 + i, c * 4 + (i + 1 - 2 * c) % 4) for c in range(2) for i in range(4)]
    blocks = [left_values[0]]
    for _ in range(3):
        blocks.append(lax.ppermute(blocks[-1], ("core", "y"), ring))

    right = mask_right(right_values[0], right_pattern[0])
    right = to_all(right.reshape(64, 32, 128), ("xl", "core"))
    right = to_all(right, ("z", "xh", "y"))
    right_far = swap(right, "xl")
    parts = (right, right_far, swap(right, "core"), swap(right_far, "core"))
    high, low = prepare(where, parts)

    send = partial_product(where, pattern, blocks, high, low, 1, (1,))
    both = partial_product(where, pattern, blocks, high, low, 0, (0, 1))
    keep = partial_product(where, pattern, blocks, high, low, 1, (0,))
    got = swap(send, "xh")
    first = lax.psum_scatter(both, "z", scatter_dimension=0, tiled=True)[0]
    second = lax.psum_scatter(keep + got, "z", scatter_dimension=0, tiled=True)[0, 0]
    first = first[0] + swap(first[1], "xh")
    return assemble(to_all(first, "y"), to_all(second, "y"))


def solution(mesh):
    fine = Mesh(mesh.devices.reshape(2, 2, 8, 2, 4), ("xl", "core", "z", "xh", "y"))
    spec = P("y", ("xl", "core"), ("z", "xh"))
    return jax.shard_map(
        body,
        mesh=fine,
        in_specs=(spec,) * 4,
        out_specs=P(("xl", "core", "y"), ("z", "xh")),
        check_vma=False,
    )
```

```python
import jax
import jax.numpy as jnp
from jax import lax
from jax.experimental import pallas as pl
from jax.experimental.pallas import tpu as pltpu
from jax.sharding import Mesh, PartitionSpec as P

BS = 128
F32 = jnp.float32
BF16 = jnp.bfloat16
VMEM_BYTES = 56 * 1024 * 1024


LIGHT = pl.CostEstimate(flops=1, bytes_accessed=1, transcendentals=0)


def mask_right_kernel(pattern_ref, values_ref, out_ref):
    at = pl.program_id(0)
    for h in range(4):
        for j in range(2):
            keep = pattern_ref[(2 * at + h // 2) * 2 + j].astype(F32)
            for i in range(2):
                columns = slice(j * BS + i * 64, j * BS + i * 64 + 64)
                top = values_ref[h * 64 : h * 64 + 32, columns]
                bottom = values_ref[h * 64 + 32 : h * 64 + 64, columns]
                out_ref[h, 0, 2 * j + i] = jnp.concatenate([top, bottom], axis=1) * keep


def mask_right(values, pattern):
    return pl.pallas_call(
        mask_right_kernel,
        grid=(4,),
        in_specs=[
            pl.BlockSpec(memory_space=pltpu.SMEM),
            pl.BlockSpec((256, 256), lambda i: (i, 0)),
        ],
        out_specs=pl.BlockSpec((4, 1, 4, 32, 128), lambda i: (0, i, 0, 0, 0)),
        out_shape=jax.ShapeDtypeStruct((4, 4, 4, 32, 128), F32),
        cost_estimate=LIGHT,
    )(pattern.reshape(16), values)


def split(block):
    high = block.astype(BF16)
    return high, (block - high.astype(F32)).astype(BF16)


def prepare_kernel(where_ref, b0_ref, b1_ref, high_ref, low_ref):
    core, xh, z = where_ref[4], where_ref[6], where_ref[7]
    for i, ref in enumerate((b0_ref, b1_ref)):
        base = lax.bitwise_xor(core, jnp.int32(i)) * 64
        for near in range(2):
            nx = lax.bitwise_xor(xh, jnp.int32(near))
            for pair in range(4):
                even = ref[lax.bitwise_and(z + 2 * pair, 7), nx, 0]
                odd = ref[lax.bitwise_and(z + 2 * pair + 1, 7), nx, 0]
                columns = slice(pair * 256 + near * 128, pair * 256 + near * 128 + 128)
                for half in range(2):
                    lanes = slice(half * 64, half * 64 + 64)
                    high, low = split(jnp.concatenate([even[:, lanes], odd[:, lanes]], axis=1))
                    rows = pl.ds(pl.multiple_of(base + half * 32, 32), 32)
                    high_ref[rows, columns] = high
                    low_ref[rows, columns] = low


def prepare(where, mine, other):
    spec = pl.BlockSpec((8, 2, 1, 32, 128), lambda t, s: (0, 0, s[t], 0, 0))
    out = pl.BlockSpec((128, 1024), lambda t, s: (t, 0))
    return pl.pallas_call(
        prepare_kernel,
        grid_spec=pltpu.PrefetchScalarGridSpec(
            num_scalar_prefetch=1, grid=(4,), in_specs=[spec] * 2, out_specs=[out] * 2
        ),
        out_shape=[jax.ShapeDtypeStruct((512, 1024), BF16)] * 2,
        cost_estimate=LIGHT,
    )(where, mine.reshape(8, 2, 4, 32, 128), other.reshape(8, 2, 4, 32, 128))


def split_kernel(block_ref, high_ref, low_ref):
    high_ref[...], low_ref[...] = split(block_ref[...])


def split_block(block):
    spec = pl.BlockSpec((2, 512, 256), lambda i: (i, 0, 0))
    return pl.pallas_call(
        split_kernel,
        grid=(2,),
        in_specs=[spec],
        out_specs=[spec] * 2,
        out_shape=[jax.ShapeDtypeStruct((4, 512, 256), BF16)] * 2,
        cost_estimate=LIGHT,
    )(block.reshape(4, 512, 256))


def product_kernel(count, where_ref, *refs):
    weights, blocks, out_ref = refs[: 4 * count], refs[4 * count : -1], refs[-1]
    sides = []
    for far in range(2):
        lanes = pl.ds(pl.multiple_of(lax.bitwise_xor(where_ref[5], jnp.int32(far)) * BS, BS), BS)
        sides.append([jnp.concatenate([ref[0, :, lanes] for ref in blocks[i::2]], axis=1) for i in range(2)])
    for at in range(count):
        terms = jnp.zeros((512, 256), F32)
        for far, (high, low) in enumerate(sides):
            w_high, w_low = (ref[...] for ref in weights[4 * at + 2 * far : 4 * at + 2 * far + 2])
            terms += jnp.dot(low, w_high, preferred_element_type=F32)
            terms += jnp.dot(high, w_low, preferred_element_type=F32)
            terms += jnp.dot(high, w_high, preferred_element_type=F32)
        for near in range(2):
            for odd in range(2):
                lanes = slice(near * 128 + odd * 64, near * 128 + odd * 64 + 64)
                out_ref[2 * at + odd, near, 0] = jnp.concatenate([terms[:256, lanes], terms[256:, lanes]], axis=1)


def partial_product(where, weights, blocks, pairs):
    n = 2 * len(pairs)
    block = pl.BlockSpec((1, 512, 256), lambda i, s: (lax.bitwise_and(s[8] + i, 3), 0, 0))
    columns = []
    for pair in pairs:
        columns += [pl.BlockSpec((512, 256), lambda i, s, pair=pair: (0, pair))] * 4
    return pl.pallas_call(
        lambda *refs: product_kernel(len(pairs), *refs),
        grid_spec=pltpu.PrefetchScalarGridSpec(
            num_scalar_prefetch=1,
            grid=(4,),
            in_specs=columns + [block] * 8,
            out_specs=pl.BlockSpec((n, 2, 1, 256, 128), lambda i, s: (0, 0, i, 0, 0)),
        ),
        out_shape=jax.ShapeDtypeStruct((n, 2, 4, 256, 128), F32),
        compiler_params=pltpu.CompilerParams(vmem_limit_bytes=VMEM_BYTES),
        cost_estimate=LIGHT,
    )(where, *(weights * len(pairs)), *blocks)


def assemble_kernel(where_ref, p0_ref, p1_ref, p2_ref, p3_ref, out_ref, held):
    for t, ref in enumerate((p0_ref, p1_ref, p2_ref, p3_ref)):
        held[lax.bitwise_and(where_ref[8] + 4 - t, 3)] = ref[...]
    for half in range(2):
        lanes = slice(half * 64, half * 64 + 64)
        for pair in range(2):
            both = jnp.concatenate([held[2 * pair, :, lanes], held[2 * pair + 1, :, lanes]], axis=1)
            out_ref[half * 256 : half * 256 + 256, pair * 128 : pair * 128 + 128] = both


def assemble(where, pieces):
    return pl.pallas_call(
        assemble_kernel,
        in_specs=[pl.BlockSpec(memory_space=pltpu.SMEM)] + [pl.BlockSpec(memory_space=pltpu.VMEM)] * 4,
        out_specs=pl.BlockSpec(memory_space=pltpu.VMEM),
        out_shape=jax.ShapeDtypeStruct((512, 256), F32),
        scratch_shapes=[pltpu.VMEM((4, 256, 128), F32)],
        cost_estimate=LIGHT,
    )(where, *pieces)


def swap(value, axis):
    return lax.ppermute(value, axis, [(0, 1), (1, 0)])


def to_all(value, axis):
    return lax.all_to_all(value, axis, split_axis=0, concat_axis=0, tiled=True)


def shift(value, axis, size, step):
    return lax.ppermute(value, axis, [(i, (i + step) % size) for i in range(size)])


def tie(*values):
    return lax.optimization_barrier(values)


def send_both(right, left):
    return shift(right, "z", 8, 1), shift(left, "z", 8, -1)


def sum_over_z(ahead, behind):
    def first(own):
        return send_both(own(4)[:2], own(4)[2:])

    def second(own, right, left):
        return send_both(
            jnp.concatenate([own(3)[:2] + right, own(3)[2:]]), jnp.concatenate([own(5)[:2], own(5)[2:] + left])
        )

    def later(own, k, right, left):
        return send_both(own(k) + right, own(8 - k) + left)

    a = first(ahead)
    b = first(behind)
    a = second(ahead, *a)
    b = second(behind, *b)
    a = later(ahead, 2, *a)
    a, b = tie(a, b)
    a = later(ahead, 1, *a)
    b = later(behind, 2, *b)
    a, b = tie(a, b)
    away = swap(ahead(0) + a[0] + a[1], "xh")
    b = later(behind, 1, *b)
    return behind(0) + b[0] + b[1] + away


def body(left_values, left_pattern, right_values, right_pattern):
    xl, core, xh, y, z = (lax.axis_index(n) for n in ("xl", "core", "xh", "y", "z"))
    turn = 1 - 2 * core
    where = jnp.stack([(y - turn * t + 4) % 4 for t in range(4)] + [core, xl, xh, z, y]).astype(jnp.int32)
    ring = [(c * 4 + i, c * 4 + (i + 1 - 2 * c) % 4) for c in range(2) for i in range(4)]

    keep = jnp.repeat(left_pattern[0].astype(F32), BS, axis=1)
    left = (left_values[0].reshape(16, BS, 256) * keep[:, None, :]).reshape(2048, 256)
    left, right_values, where = tie(left, right_values, where)
    left1 = lax.ppermute(left, ("core", "y"), ring)

    right = mask_right(right_values[0], right_pattern[0])
    right = to_all(right.reshape(64, 32, 128), ("xl", "core"))
    left1, right = tie(left1, right)
    left2 = lax.ppermute(left1, ("core", "y"), ring)
    right = to_all(right, ("z", "xh", "y"))
    left2, right = tie(left2, right)
    left3 = lax.ppermute(left2, ("core", "y"), ring)
    blocks = (left, left1, left2, left3)
    right_far = swap(right, "xl")
    weights = prepare(where, right, swap(right, "core"))
    halves = [half for block in blocks[:3] for half in split_block(block)]
    right_far, weights, halves = tie(right_far, weights, halves)
    halves += split_block(blocks[3])
    weights = (*weights, *prepare(where, right_far, swap(right_far, "core")))

    middle = partial_product(where, weights, halves, (2,))
    weights, middle = tie(weights, middle)
    third = partial_product(where, weights, halves, (1,))
    weights, third = tie(weights, third)
    others = partial_product(where, weights, halves, (0, 3))
    chunks = [others[0], others[1], third[0], third[1], middle[0], middle[1], others[2], others[3]]
    mine = sum_over_z(lambda k: chunks[k][1], lambda k: chunks[k][0])
    pieces = [mine[0]] + [shift(mine[t], "y", 4, t) for t in (1, 2, 3)]
    return assemble(where, pieces)


def solution(mesh):
    fine = Mesh(mesh.devices.reshape(2, 2, 8, 2, 4), ("xl", "core", "z", "xh", "y"))
    spec = P("y", ("xl", "core"), ("z", "xh"))
    return jax.shard_map(
        body,
        mesh=fine,
        in_specs=(spec,) * 4,
        out_specs=P(("xl", "core", "y"), ("z", "xh")),
        check_vma=False,
    )
```

```python
import jax
import jax.numpy as jnp
from jax import lax
from jax.experimental import pallas as pl
from jax.experimental.pallas import tpu as pltpu
from jax.sharding import Mesh, PartitionSpec as P

BS = 128
F32 = jnp.float32
BF16 = jnp.bfloat16
VMEM_BYTES = 20 * 1024 * 1024


LIGHT = pl.CostEstimate(flops=1, bytes_accessed=1, transcendentals=0)


def mask_right_kernel(pattern_ref, values_ref, out_ref):
    for g in range(2):
        at = 2 * pl.program_id(0) + g
        for h in range(4):
            start = g * 256 + h * 64
            for j in range(2):
                keep = pattern_ref[(2 * at + h // 2) * 2 + j].astype(F32)
                columns = slice(j * BS, (j + 1) * BS)
                top = values_ref[start : start + 32, columns] * keep
                bottom = values_ref[start + 32 : start + 64, columns] * keep
                for i in range(2):
                    lanes = slice(i * 64, i * 64 + 64)
                    out_ref[h, g, 2 * j + i] = jnp.concatenate([top[:, lanes], bottom[:, lanes]], axis=1)


def mask_right(values, pattern):
    return pl.pallas_call(
        mask_right_kernel,
        grid=(2,),
        in_specs=[
            pl.BlockSpec(memory_space=pltpu.SMEM),
            pl.BlockSpec((512, 256), lambda i: (i, 0)),
        ],
        out_specs=pl.BlockSpec((4, 2, 4, 32, 128), lambda i: (0, i, 0, 0, 0)),
        out_shape=jax.ShapeDtypeStruct((4, 4, 4, 32, 128), F32),
        compiler_params=pltpu.CompilerParams(vmem_limit_bytes=VMEM_BYTES),
        cost_estimate=LIGHT,
    )(pattern.reshape(16), values)


def split(block):
    high = block.astype(BF16)
    return high, (block - high.astype(F32)).astype(BF16)


def prepare_kernel(where_ref, b0_ref, b1_ref, high_ref, low_ref):
    core, xh, z = where_ref[4], where_ref[6], where_ref[7]
    for t in range(4):
        ky = where_ref[t]
        for i, ref in enumerate((b0_ref, b1_ref)):
            base = t * BS + lax.bitwise_xor(core, jnp.int32(i)) * 64
            rows = pl.ds(pl.multiple_of(base, 64), 64)
            for near in range(2):
                nx = lax.bitwise_xor(xh, jnp.int32(near))
                for pair in range(4):
                    even = ref[lax.bitwise_and(z + 2 * pair, 7), nx, ky]
                    odd = ref[lax.bitwise_and(z + 2 * pair + 1, 7), nx, ky]
                    top = jnp.concatenate([even[:, :64], odd[:, :64]], axis=1)
                    bottom = jnp.concatenate([even[:, 64:], odd[:, 64:]], axis=1)
                    columns = slice(pair * 256 + near * 128, pair * 256 + near * 128 + 128)
                    high, low = split(jnp.concatenate([top, bottom], axis=0))
                    high_ref[rows, columns] = high
                    low_ref[rows, columns] = low


def prepare(where, mine, other):
    whole = pl.BlockSpec(memory_space=pltpu.VMEM)
    return pl.pallas_call(
        prepare_kernel,
        in_specs=[pl.BlockSpec(memory_space=pltpu.SMEM), whole, whole],
        out_specs=[whole] * 2,
        out_shape=[jax.ShapeDtypeStruct((512, 1024), BF16)] * 2,
        compiler_params=pltpu.CompilerParams(vmem_limit_bytes=VMEM_BYTES),
        cost_estimate=LIGHT,
    )(where, mine.reshape(8, 2, 4, 32, 128), other.reshape(8, 2, 4, 32, 128))


def split_kernel(block_ref, high_ref, low_ref):
    high_ref[...], low_ref[...] = split(block_ref[...])


def split_block(block):
    spec = pl.BlockSpec((2, 512, 256), lambda i: (i, 0, 0))
    return pl.pallas_call(
        split_kernel,
        grid=(2,),
        in_specs=[spec],
        out_specs=[spec] * 2,
        out_shape=[jax.ShapeDtypeStruct((4, 512, 256), BF16)] * 2,
        compiler_params=pltpu.CompilerParams(vmem_limit_bytes=VMEM_BYTES),
        cost_estimate=LIGHT,
    )(block.reshape(4, 512, 256))


def product_kernel(count, where_ref, *refs):
    weights, blocks, last_ref, outs = refs[: 4 * count], refs[4 * count : 4 * count + 6], refs[4 * count + 6], refs[4 * count + 7 :]
    sides = []
    for far in range(2):
        lanes = pl.ds(pl.multiple_of(lax.bitwise_xor(where_ref[5], jnp.int32(far)) * BS, BS), BS)
        last = split(last_ref[0, :, lanes])
        sides.append(
            [jnp.concatenate([ref[0, :, lanes] for ref in blocks[i::2]] + [last[i]], axis=1) for i in range(2)]
        )
    for at in range(count):
        terms = jnp.zeros((512, 256), F32)
        for far, (high, low) in enumerate(sides):
            w_high, w_low = (ref[...] for ref in weights[4 * at + 2 * far : 4 * at + 2 * far + 2])
            terms += jnp.dot(low, w_high, preferred_element_type=F32)
            terms += jnp.dot(high, w_low, preferred_element_type=F32)
            terms += jnp.dot(high, w_high, preferred_element_type=F32)
        for near in range(2):
            for odd in range(2):
                lanes = slice(near * 128 + odd * 64, near * 128 + odd * 64 + 64)
                packed = jnp.concatenate([terms[:256, lanes], terms[256:, lanes]], axis=1)
                if len(outs) == 1:
                    outs[0][2 * at + odd, near, 0] = packed
                elif odd == 1:
                    outs[0][near, 0] = packed
                else:
                    for half in range(2):

                        @pl.when(pl.program_id(0) // 2 == half)
                        def _():
                            outs[1 + 2 * near + half][0] = packed


def partial_product(where, weights, blocks, last, pairs, apart=False):
    n = 2 * len(pairs)
    block = pl.BlockSpec((1, 512, 256), lambda i, s: (lax.bitwise_and(s[8] + i, 3), 0, 0))
    columns = []
    for pair in pairs:
        columns += [pl.BlockSpec((512, 256), lambda i, s, pair=pair: (0, pair))] * 4
    if apart:
        out_specs = [pl.BlockSpec((2, 1, 256, 128), lambda i, s: (0, i, 0, 0))]
        out_specs += [
            pl.BlockSpec((1, 256, 128), lambda i, s: (jnp.minimum(i, 1), 0, 0)),
            pl.BlockSpec((1, 256, 128), lambda i, s: (jnp.maximum(i - 2, 0), 0, 0)),
        ] * 2
        out_shape = [jax.ShapeDtypeStruct((2, 4, 256, 128), F32)] + [jax.ShapeDtypeStruct((2, 256, 128), F32)] * 4
    else:
        out_specs = pl.BlockSpec((n, 2, 1, 256, 128), lambda i, s: (0, 0, i, 0, 0))
        out_shape = jax.ShapeDtypeStruct((n, 2, 4, 256, 128), F32)
    return pl.pallas_call(
        lambda *refs: product_kernel(len(pairs), *refs),
        grid_spec=pltpu.PrefetchScalarGridSpec(
            num_scalar_prefetch=1,
            grid=(4,),
            in_specs=columns + [block] * 7,
            out_specs=out_specs,
        ),
        out_shape=out_shape,
        compiler_params=pltpu.CompilerParams(vmem_limit_bytes=VMEM_BYTES),
        cost_estimate=LIGHT,
    )(where, *(weights * len(pairs)), *blocks, last.reshape(4, 512, 256))


def assemble_kernel(where_ref, p0_ref, p1_ref, p2_ref, p3_ref, out_ref, held):
    for t, ref in enumerate((p0_ref, p1_ref, p2_ref, p3_ref)):
        held[lax.bitwise_and(where_ref[8] + 4 - t, 3)] = ref[...]
    for half in range(2):
        lanes = slice(half * 64, half * 64 + 64)
        for pair in range(2):
            both = jnp.concatenate([held[2 * pair, :, lanes], held[2 * pair + 1, :, lanes]], axis=1)
            out_ref[half * 256 : half * 256 + 256, pair * 128 : pair * 128 + 128] = both


def assemble(where, pieces):
    return pl.pallas_call(
        assemble_kernel,
        in_specs=[pl.BlockSpec(memory_space=pltpu.SMEM)] + [pl.BlockSpec(memory_space=pltpu.VMEM)] * 4,
        out_specs=pl.BlockSpec(memory_space=pltpu.VMEM),
        out_shape=jax.ShapeDtypeStruct((512, 256), F32),
        scratch_shapes=[pltpu.VMEM((4, 256, 128), F32)],
        cost_estimate=LIGHT,
    )(where, *pieces)


def swap(value, axis):
    return lax.ppermute(value, axis, [(0, 1), (1, 0)])


def to_all(value, axis):
    return lax.all_to_all(value, axis, split_axis=0, concat_axis=0, tiled=True)


def shift(value, axis, size, step):
    return lax.ppermute(value, axis, [(i, (i + step) % size) for i in range(size)])


def tie(*values):
    return lax.optimization_barrier(values)


def send_both(right, left):
    return shift(right, "z", 8, 1), shift(left, "z", 8, -1)


def sum_over_z(ahead, behind):
    def first(own):
        return send_both(*own(4))

    def second(own, right, left):
        return send_both(
            jnp.concatenate([own(3)[:2] + right, own(3)[2:]]), jnp.concatenate([own(5)[:2], own(5)[2:] + left])
        )

    def later(own, k, right, left):
        return send_both(own(k) + right, own(8 - k) + left)

    a = first(ahead)
    b = first(behind)
    a = second(ahead, *a)
    b = second(behind, *b)
    a = later(ahead, 2, *a)
    a, b = tie(a, b)
    a = later(ahead, 1, *a)
    b = later(behind, 2, *b)
    a, b = tie(a, b)
    away = swap(ahead(0) + a[0] + a[1], "xh")
    b = later(behind, 1, *b)
    return behind(0) + b[0] + b[1] + away


def body(left_values, left_pattern, right_values, right_pattern):
    xl, core, xh, y, z = (lax.axis_index(n) for n in ("xl", "core", "xh", "y", "z"))
    turn = 1 - 2 * core
    where = jnp.stack([(y - turn * t + 4) % 4 for t in range(4)] + [core, xl, xh, z, y]).astype(jnp.int32)
    ring = [(c * 4 + i, c * 4 + (i + 1 - 2 * c) % 4) for c in range(2) for i in range(4)]

    keep = jnp.repeat(left_pattern[0].astype(F32), BS, axis=1)
    left = (left_values[0].reshape(16, BS, 256) * keep[:, None, :]).reshape(2048, 256)
    left, right_values, where = tie(left, right_values, where)
    left1 = lax.ppermute(left, ("core", "y"), ring)

    right = mask_right(right_values[0], right_pattern[0])
    right = to_all(right.reshape(64, 32, 128), ("xl", "core"))
    left1, right = tie(left1, right)
    left2 = lax.ppermute(left1, ("core", "y"), ring)
    right = to_all(right, ("z", "xh", "y"))
    left2, right = tie(left2, right)
    left3 = lax.ppermute(left2, ("core", "y"), ring)
    blocks = (left, left1, left2, left3)
    right_far = swap(right, "xl")
    weights = prepare(where, right, swap(right, "core"))
    halves = [half for block in blocks[:3] for half in split_block(block)]
    right_far, weights, halves = tie(right_far, weights, halves)
    weights = (*weights, *prepare(where, right_far, swap(right_far, "core")))

    fifth, *fourth = partial_product(where, weights, halves, left3, (2,), True)
    weights, fifth = tie(weights, fifth)
    third = partial_product(where, weights, halves, left3, (1,))
    weights, third = tie(weights, third)
    others = partial_product(where, weights, halves, left3, (0, 3))
    chunks = [others[0], others[1], third[0], third[1], (fourth[:2], fourth[2:]), fifth, others[2], others[3]]
    mine = sum_over_z(lambda k: chunks[k][1], lambda k: chunks[k][0])
    pieces = [mine[0]] + [shift(mine[t], "y", 4, t) for t in (1, 2, 3)]
    return assemble(where, pieces)


def solution(mesh):
    fine = Mesh(mesh.devices.reshape(2, 2, 8, 2, 4), ("xl", "core", "z", "xh", "y"))
    spec = P("y", ("xl", "core"), ("z", "xh"))
    return jax.shard_map(
        body,
        mesh=fine,
        in_specs=(spec,) * 4,
        out_specs=P(("xl", "core", "y"), ("z", "xh")),
        check_vma=False,
    )
```

```python
import jax
import jax.numpy as jnp
from jax import lax
from jax.experimental import pallas as pl
from jax.experimental.pallas import tpu as pltpu
from jax.sharding import Mesh, PartitionSpec as P

BS = 128
F32 = jnp.float32
BF16 = jnp.bfloat16
VMEM_BYTES = 20 * 1024 * 1024


LIGHT = pl.CostEstimate(flops=1, bytes_accessed=1, transcendentals=0)


def mask_right_kernel(pattern_ref, values_ref, out_ref):
    for g in range(2):
        at = 2 * pl.program_id(0) + g
        for h in range(4):
            start = g * 256 + h * 64
            for j in range(2):
                keep = pattern_ref[(2 * at + h // 2) * 2 + j].astype(F32)
                columns = slice(j * BS, (j + 1) * BS)
                top = values_ref[start : start + 32, columns] * keep
                bottom = values_ref[start + 32 : start + 64, columns] * keep
                for i in range(2):
                    lanes = slice(i * 64, i * 64 + 64)
                    out_ref[h, g, 2 * j + i] = jnp.concatenate([top[:, lanes], bottom[:, lanes]], axis=1)


def mask_right(values, pattern):
    return pl.pallas_call(
        mask_right_kernel,
        grid=(2,),
        in_specs=[
            pl.BlockSpec(memory_space=pltpu.SMEM),
            pl.BlockSpec((512, 256), lambda i: (i, 0)),
        ],
        out_specs=pl.BlockSpec((4, 2, 4, 32, 128), lambda i: (0, i, 0, 0, 0)),
        out_shape=jax.ShapeDtypeStruct((4, 4, 4, 32, 128), F32),
        compiler_params=pltpu.CompilerParams(vmem_limit_bytes=VMEM_BYTES),
        cost_estimate=LIGHT,
    )(pattern.reshape(16), values)


def split(block):
    high = block.astype(BF16)
    return high, (block - high.astype(F32)).astype(BF16)


def prepare_kernel(where_ref, b0_ref, b1_ref, high_ref, low_ref):
    core, xh, z = where_ref[4], where_ref[6], where_ref[7]
    for t in range(4):
        ky = where_ref[t]
        for i, ref in enumerate((b0_ref, b1_ref)):
            base = t * BS + lax.bitwise_xor(core, jnp.int32(i)) * 64
            rows = pl.ds(pl.multiple_of(base, 64), 64)
            for near in range(2):
                nx = lax.bitwise_xor(xh, jnp.int32(near))
                for pair in range(4):
                    even = ref[lax.bitwise_and(z + 2 * pair, 7), nx, ky]
                    odd = ref[lax.bitwise_and(z + 2 * pair + 1, 7), nx, ky]
                    top = jnp.concatenate([even[:, :64], odd[:, :64]], axis=1)
                    bottom = jnp.concatenate([even[:, 64:], odd[:, 64:]], axis=1)
                    columns = slice(pair * 256 + near * 128, pair * 256 + near * 128 + 128)
                    high, low = split(jnp.concatenate([top, bottom], axis=0))
                    high_ref[rows, columns] = high
                    low_ref[rows, columns] = low


def prepare(where, mine, other):
    whole = pl.BlockSpec(memory_space=pltpu.VMEM)
    return pl.pallas_call(
        prepare_kernel,
        in_specs=[pl.BlockSpec(memory_space=pltpu.SMEM), whole, whole],
        out_specs=[whole] * 2,
        out_shape=[jax.ShapeDtypeStruct((512, 1024), BF16)] * 2,
        compiler_params=pltpu.CompilerParams(vmem_limit_bytes=VMEM_BYTES),
        cost_estimate=LIGHT,
    )(where, mine.reshape(8, 2, 4, 32, 128), other.reshape(8, 2, 4, 32, 128))


def split_kernel(block_ref, high_ref, low_ref):
    high_ref[...], low_ref[...] = split(block_ref[...])


def split_block(block):
    spec = pl.BlockSpec((2, 512, 256), lambda i: (i, 0, 0))
    return pl.pallas_call(
        split_kernel,
        grid=(2,),
        in_specs=[spec],
        out_specs=[spec] * 2,
        out_shape=[jax.ShapeDtypeStruct((4, 512, 256), BF16)] * 2,
        compiler_params=pltpu.CompilerParams(vmem_limit_bytes=VMEM_BYTES),
        cost_estimate=LIGHT,
    )(block.reshape(4, 512, 256))


def product_kernel(count, where_ref, *refs):
    weights, blocks, last_ref, outs = refs[: 4 * count], refs[4 * count : 4 * count + 6], refs[4 * count + 6], refs[4 * count + 7 :]
    sides = []
    for far in range(2):
        lanes = pl.ds(pl.multiple_of(lax.bitwise_xor(where_ref[5], jnp.int32(far)) * BS, BS), BS)
        last = split(last_ref[0, :, lanes])
        sides.append(
            [jnp.concatenate([ref[0, :, lanes] for ref in blocks[i::2]] + [last[i]], axis=1) for i in range(2)]
        )
    for at in range(count):
        terms = jnp.zeros((512, 256), F32)
        for far, (high, low) in enumerate(sides):
            w_high, w_low = (ref[...] for ref in weights[4 * at + 2 * far : 4 * at + 2 * far + 2])
            terms += jnp.dot(low, w_high, preferred_element_type=F32)
            terms += jnp.dot(high, w_low, preferred_element_type=F32)
            terms += jnp.dot(high, w_high, preferred_element_type=F32)
        for near in range(2):
            for odd in range(2):
                lanes = slice(near * 128 + odd * 64, near * 128 + odd * 64 + 64)
                packed = jnp.concatenate([terms[:256, lanes], terms[256:, lanes]], axis=1)
                if len(outs) == 1:
                    outs[0][2 * at + odd, near, 0] = packed
                elif odd == 1:
                    outs[0][near, 0] = packed
                else:
                    for half in range(2):

                        @pl.when(pl.program_id(0) // 2 == half)
                        def _():
                            outs[1 + 2 * near + half][0] = packed


def partial_product(where, weights, blocks, last, pairs, apart=False):
    n = 2 * len(pairs)
    block = pl.BlockSpec((1, 512, 256), lambda i, s: (lax.bitwise_and(s[8] + i, 3), 0, 0))
    columns = []
    for pair in pairs:
        columns += [pl.BlockSpec((512, 256), lambda i, s, pair=pair: (0, pair))] * 4
    if apart:
        out_specs = [pl.BlockSpec((2, 1, 256, 128), lambda i, s: (0, i, 0, 0))]
        out_specs += [
            pl.BlockSpec((1, 256, 128), lambda i, s: (jnp.minimum(i, 1), 0, 0)),
            pl.BlockSpec((1, 256, 128), lambda i, s: (jnp.maximum(i - 2, 0), 0, 0)),
        ] * 2
        out_shape = [jax.ShapeDtypeStruct((2, 4, 256, 128), F32)] + [jax.ShapeDtypeStruct((2, 256, 128), F32)] * 4
    else:
        out_specs = pl.BlockSpec((n, 2, 1, 256, 128), lambda i, s: (0, 0, i, 0, 0))
        out_shape = jax.ShapeDtypeStruct((n, 2, 4, 256, 128), F32)
    return pl.pallas_call(
        lambda *refs: product_kernel(len(pairs), *refs),
        grid_spec=pltpu.PrefetchScalarGridSpec(
            num_scalar_prefetch=1,
            grid=(4,),
            in_specs=columns + [block] * 7,
            out_specs=out_specs,
        ),
        out_shape=out_shape,
        compiler_params=pltpu.CompilerParams(vmem_limit_bytes=VMEM_BYTES),
        cost_estimate=LIGHT,
    )(where, *(weights * len(pairs)), *blocks, last.reshape(4, 512, 256))


def assemble_kernel(where_ref, p0_ref, p1_ref, p2_ref, p3_ref, out_ref, held):
    for t, ref in enumerate((p0_ref, p1_ref, p2_ref, p3_ref)):
        held[lax.bitwise_and(where_ref[8] + 4 - t, 3)] = ref[...]
    for half in range(2):
        lanes = slice(half * 64, half * 64 + 64)
        for pair in range(2):
            both = jnp.concatenate([held[2 * pair, :, lanes], held[2 * pair + 1, :, lanes]], axis=1)
            out_ref[half * 256 : half * 256 + 256, pair * 128 : pair * 128 + 128] = both


def assemble(where, pieces):
    return pl.pallas_call(
        assemble_kernel,
        in_specs=[pl.BlockSpec(memory_space=pltpu.SMEM)] + [pl.BlockSpec(memory_space=pltpu.VMEM)] * 4,
        out_specs=pl.BlockSpec(memory_space=pltpu.VMEM),
        out_shape=jax.ShapeDtypeStruct((512, 256), F32),
        scratch_shapes=[pltpu.VMEM((4, 256, 128), F32)],
        compiler_params=pltpu.CompilerParams(vmem_limit_bytes=VMEM_BYTES),
        cost_estimate=LIGHT,
    )(where, *pieces)


def swap(value, axis):
    return lax.ppermute(value, axis, [(0, 1), (1, 0)])


def to_all(value, axis):
    return lax.all_to_all(value, axis, split_axis=0, concat_axis=0, tiled=True)


def shift(value, axis, size, step):
    return lax.ppermute(value, axis, [(i, (i + step) % size) for i in range(size)])


def tie(*values):
    return lax.optimization_barrier(values)


def send_both(right, left):
    return shift(right, "z", 8, 1), shift(left, "z", 8, -1)


def sum_over_z(ahead, behind):
    def first(own):
        return send_both(*own(4))

    def second(own, right, left):
        return send_both(
            jnp.concatenate([own(3)[:2] + right, own(3)[2:]]), jnp.concatenate([own(5)[:2], own(5)[2:] + left])
        )

    def later(own, k, right, left):
        return send_both(own(k) + right, own(8 - k) + left)

    a = first(ahead)
    b = first(behind)
    a = second(ahead, *a)
    b = second(behind, *b)
    a = later(ahead, 2, *a)
    a, b = tie(a, b)
    a = later(ahead, 1, *a)
    b = later(behind, 2, *b)
    a, b = tie(a, b)
    away = swap(ahead(0) + a[0] + a[1], "xh")
    b = later(behind, 1, *b)
    return behind(0) + b[0] + b[1] + away


def body(left_values, left_pattern, right_values, right_pattern):
    xl, core, xh, y, z = (lax.axis_index(n) for n in ("xl", "core", "xh", "y", "z"))
    turn = 1 - 2 * core
    where = jnp.stack([(y - turn * t + 4) % 4 for t in range(4)] + [core, xl, xh, z, y]).astype(jnp.int32)
    ring = [(c * 4 + i, c * 4 + (i + 1 - 2 * c) % 4) for c in range(2) for i in range(4)]

    left = left_values[0].reshape(16, BS, 2, BS) * left_pattern[0].astype(F32)[:, None, :, None]
    left = left.reshape(2048, 256)
    left, right_values, where = tie(left, right_values, where)
    left1 = lax.ppermute(left, ("core", "y"), ring)

    right = mask_right(right_values[0], right_pattern[0])
    right = to_all(right.reshape(64, 32, 128), ("xl", "core"))
    left1, right = tie(left1, right)
    left2 = lax.ppermute(left1, ("core", "y"), ring)
    right = to_all(right, ("z", "xh", "y"))
    left2, right = tie(left2, right)
    left3 = lax.ppermute(left2, ("core", "y"), ring)
    blocks = (left, left1, left2, left3)
    right_far = swap(right, "xl")
    weights = prepare(where, right, swap(right, "core"))
    halves = [half for block in blocks[:3] for half in split_block(block)]
    right_far, weights, halves = tie(right_far, weights, halves)
    weights = (*weights, *prepare(where, right_far, swap(right_far, "core")))

    fifth, *fourth = partial_product(where, weights, halves, left3, (2,), True)
    weights, fifth = tie(weights, fifth)
    others = partial_product(where, weights, halves, left3, (0, 1, 3))
    chunks = [others[0], others[1], others[2], others[3], (fourth[:2], fourth[2:]), fifth, others[4], others[5]]
    mine = sum_over_z(lambda k: chunks[k][1], lambda k: chunks[k][0])
    pieces = [mine[0]] + [shift(mine[t], "y", 4, t) for t in (1, 2, 3)]
    return assemble(where, pieces)


def solution(mesh):
    fine = Mesh(mesh.devices.reshape(2, 2, 8, 2, 4), ("xl", "core", "z", "xh", "y"))
    spec = P("y", ("xl", "core"), ("z", "xh"))
    return jax.shard_map(
        body,
        mesh=fine,
        in_specs=(spec,) * 4,
        out_specs=P(("xl", "core", "y"), ("z", "xh")),
        check_vma=False,
    )
```
